32 devices in a mesh: dp: 8 (over y, x, core), seq: 4 (over z).
Axes of the slice: x: 2, y: 2, z: 4, core: 2. Of those that a mesh axis runs over, the one named last changes fastest.
Arguments:
- hidden_in: bfloat16 [8192, 2048], P(('dp', 'seq')), may hold values from -6 to 6
- mix_values: bfloat16 [8192, 4096], P(('dp', 'seq')), may hold values from -6 to 6
- mix_gate: bfloat16 [8192, 4096], P(('dp', 'seq')), may hold values from -6 to 6
- state_proj: bfloat16 [8192, 2048], P(('dp', 'seq')), may hold values from -2 to 2
- step_raw: bfloat16 [8192, 64], P(('dp', 'seq')), may hold values from -4 to 4
- step_bias: float32 [64], replicated, may hold values from -1 to 0.5
- decay_rate: float32 [64], replicated, may hold values from 0.1 to 40
- skip_gain: float32 [64], replicated, may hold values from 0.5 to 1.5
- norm_gain: float32 [4096], replicated, may hold values from 0.5 to 1.5
- out_weight: bfloat16 [4096, 2048], P('seq'), may hold values from -0.09375 to 0.09375
- ffn_gain: float32 [2048], replicated, may hold values from 0.5 to 1.5
- expert_ids: int32 [8192, 8], P(('dp', 'seq')), may hold values from 0 to 31, all different within a row; in each aligned block of 256 rows (0 to 255, 256 to 511, ...) at most 72 rows name the same one
- route_weights: float32 [8192, 8], P(('dp', 'seq')), may hold values from 0.05 to 0.25
- gate_up: bfloat16 [32, 2048, 1536], P(('dp', 'seq')), may hold values from -0.125 to 0.125
- down_proj: bfloat16 [32, 768, 2048], P(('dp', 'seq')), may hold values from -0.21875 to 0.21875
- doc_lengths: int32 [8, 3], P('dp'), may hold values from 1 to 768, 1024 in all within a row
Outputs:
- block_out: bfloat16 [8192, 2048], P(('dp', 'seq'))
The draws below stay inside these ranges and needn't reach their ends.
Inputs may be any that keep to these rules, and one draw needn't show every extreme that they name: `expert_ids`: in the rows of one device (aligned blocks of 256 tokens) no expert is chosen more than 72 times, a bound that some block reaches; a token's 8 experts differ. `doc_lengths`: each row sums to 1024; its largest length is exactly three quarters of 1024, rounded down.
All inputs are finite; a program needn't handle non-finite values.
Results may differ from the reference program's by a relative error of at most 0.019.
Values may be sent and summed in bfloat16 or wider, within the bound.
A program may use at most 256 MiB of HBM per device.

```python
import math
import jax
import jax.numpy as jnp
import numpy as np
from jax import lax

D = 2048
HEADS = 64
HEADDIM = 64
STATE = 128
GROUPS = 8
SPAN = 256
FF = 768
TOP = 8
DOCS = 3
TOK_DEV = 256
SEQ_TOK = 1024
TOKENS = 8192
DI = 4096
EXPERTS = 32
CAP = 72
N_DP = 8


def level_of(key, extent, cuts, least, top_value):
    def one(axis_at, shards_of):
        steps = jax.random.uniform(jax.random.fold_in(jax.random.fold_in(key, 6), axis_at), (shards_of,), jnp.float32, least / len(cuts), top_value / len(cuts))
        return jnp.repeat(jnp.exp(steps), extent[axis_at] // shards_of).reshape((-1,) + (1,) * (len(extent) - axis_at - 1))

    level = one(*cuts[0])
    for cut in cuts[1:]:
        level = level * one(*cut)
    return level


def length_profile(amount, total, most, slope):
    weights = [(1 << 20) // math.isqrt(rank ** slope) + 1 for rank in range(2, amount + 1)]
    rest, given = total - most - (amount - 1), [1] * (amount - 1)
    while rest > 0:
        candidates = [i for i in range(amount - 1) if given[i] < most]
        whole, budget = sum([weights[i] for i in candidates]), rest
        for i in candidates:
            addition = min(most - given[i], max(1, budget * weights[i] // whole), rest)
            given[i] = given[i] + addition
            rest = rest - addition
    return np.array([most] + given)


def ragged(key, count, total, limit, lean):
    if count == 2:
        one = jax.random.randint(key, (), max(1, total - limit), min(limit, total - 1) + 1)
        return jnp.stack([one, total - one])
    tallies = jnp.asarray(length_profile(count, total, limit, lean), jnp.int32)
    couples = (count - 1) // 2
    donor, sink = tallies[1:1 + 2 * couples:2], tallies[2:2 + 2 * couples:2]
    slack = jnp.minimum(donor - 1, limit - sink)
    passed = jax.random.randint(jax.random.fold_in(key, 1), (couples,), 0, 1 << 20) % (slack + 1)
    tallies = tallies.at[1:1 + 2 * couples:2].set(donor - passed).at[2:2 + 2 * couples:2].set(sink + passed)
    return tallies[jax.random.permutation(jax.random.fold_in(key, 2), count)]


def shared_out(rng, own, number, rows, amount, top, bound, slope):
    sequence = jax.random.permutation(rng, amount)
    heavy_load, usual = shares(amount, rows * top, bound, slope, True), shares(amount, rows * top, bound, slope, False)
    places = jnp.arange(amount)

    def named(tallies, rotation):
        used = int((tallies > 0).sum())
        fixed = max(1, used // 4)
        moved = fixed + (places - fixed + rotation * (used - fixed)) % max(1, amount - fixed)
        return jnp.zeros((amount,), jnp.int32).at[sequence[jnp.where(places < fixed, places, moved)]].set(jnp.asarray(tallies, jnp.int32))

    tallies = jnp.where(number % 4 == 0, named(heavy_load, number // 4), named(usual, number - number // 4 - 1))
    mixed = jax.random.permutation(jax.random.fold_in(own, 3), amount)
    donor, taker = mixed[0:amount // 2 * 2:2], mixed[1:amount // 2 * 2:2]
    slack = jnp.minimum(tallies[donor] - 1, bound - tallies[taker]) // 2
    slack = jnp.where((donor == sequence[0]) | (taker == sequence[0]) | (tallies[taker] == 0), 0, jnp.maximum(slack, 0))
    moved = jax.random.randint(jax.random.fold_in(own, 4), (amount // 2,), 0, 1 << 20) % (slack + 1)
    tallies = tallies.at[donor].add(-moved).at[taker].add(moved)
    labels = jnp.searchsorted(jnp.cumsum(tallies), jnp.arange(rows * top), side="right").astype(jnp.int32)
    table = labels.reshape(top, rows).T
    table = table[jax.random.permutation(jax.random.fold_in(own, 1), rows)]
    rotation = jax.random.randint(jax.random.fold_in(own, 2), (rows, 1), 0, top)
    return jnp.take_along_axis(table, (jnp.arange(top)[None, :] + rotation) % top, axis=1)


def shares(amount, total, most, slope, full):
    loads = [(1 << 20) // math.isqrt(rank ** slope) + 1 for rank in range(1, amount + 1)]
    largest = most if full else min(most, max(-(-total // amount), total * loads[0] // sum(loads)))
    least = 1 if total - largest >= amount - 1 else 0
    holding, rest = [largest] + [least] * (amount - 1), total - largest - least * (amount - 1)
    while rest > 0:
        free = [i for i in range(1, amount) if holding[i] < largest] or [i for i in range(1, amount) if holding[i] < most]
        whole, left = sum([loads[i] for i in free]), rest
        for i in free:
            more = min(most - holding[i], max(1, left * loads[i] // whole), rest)
            holding[i] = holding[i] + more
            rest = rest - more
    return np.array(holding)


def normal_values(own_key, extent, scale, most, shards=(), kind=jnp.bfloat16):
    level = level_of(own_key, extent, shards, -0.22, 0.18) if shards else 1.0
    values = jax.random.normal(own_key, extent, jnp.float32) * scale * level
    return jnp.minimum(jnp.maximum(values, -most), most).astype(kind)


def setup_inputs(seed: int = 0) -> dict:
    streams_of = jax.random.split(jax.random.key(seed), 17)
    hidden_in = normal_values(streams_of[0], (TOKENS, D), 1.0, 6.0, ((0, 32),))
    mix_values = normal_values(streams_of[1], (TOKENS, DI), 1.0, 6.0, ((0, 32),))
    mix_gate = normal_values(streams_of[2], (TOKENS, DI), 1.0, 6.0, ((0, 32),))
    state_proj = normal_values(streams_of[3], (TOKENS, 2 * GROUPS * STATE), 0.3, 2.0, ((0, 32),))
    step_raw = normal_values(streams_of[4], (TOKENS, HEADS), 1.0, 4.0, ((0, 32),))
    step_bias = jnp.clip(jax.random.uniform(streams_of[5], (HEADS,), jnp.float32, -1.0, 0.5), -1.0, 0.5)
    decay_rate = jnp.clip(jnp.exp(jax.random.uniform(streams_of[6], (HEADS,), jnp.float32, math.log(0.1), math.log(40.0))), 0.1, 40.0)
    skip_gain = jnp.clip(jax.random.uniform(streams_of[7], (HEADS,), jnp.float32, 0.5, 1.5), 0.5, 1.5)
    norm_gain = jnp.clip(1.0 + 0.1 * jax.random.normal(streams_of[8], (DI,), jnp.float32), 0.5, 1.5)
    out_weight = normal_values(streams_of[9], (DI, D), DI ** -0.5, 0.09375, ((0, 4),))
    ffn_gain = jnp.clip(1.0 + 0.1 * jax.random.normal(streams_of[10], (D,), jnp.float32), 0.5, 1.5)
    expert_ids_keys = jax.random.split(jax.random.fold_in(streams_of[11], 1), TOKENS // TOK_DEV)
    expert_ids_turns = jax.random.permutation(jax.random.fold_in(streams_of[11], 3), TOKENS // TOK_DEV)
    expert_ids = jax.vmap(lambda own, number: shared_out(jax.random.fold_in(streams_of[11], 2), own, number, TOK_DEV, EXPERTS, TOP, CAP, 2))(expert_ids_keys, expert_ids_turns).reshape((TOKENS, TOP))
    route_weights = jnp.clip(0.05 + 0.2 * jax.random.uniform(streams_of[12], (TOKENS, TOP), jnp.float32) ** level_of(streams_of[12], (TOKENS, TOP), ((0, 32),), -0.2, 0.2), 0.05, 0.25)
    gate_up = normal_values(streams_of[13], (EXPERTS, D, 2 * FF), D ** -0.5, 0.125, ((0, 32),))
    down_proj = normal_values(streams_of[14], (EXPERTS, FF, D), FF ** -0.5, 0.21875, ((0, 32),))
    doc_lengths = jax.vmap(lambda own: ragged(own, DOCS, SEQ_TOK, SEQ_TOK * 3 // 4, 2))(jax.random.split(streams_of[15], N_DP)).reshape((N_DP, DOCS)).astype(jnp.int32)
    return {"hidden_in": hidden_in, "mix_values": mix_values, "mix_gate": mix_gate, "state_proj": state_proj, "step_raw": step_raw, "step_bias": step_bias, "decay_rate": decay_rate, "skip_gain": skip_gain, "norm_gain": norm_gain, "out_weight": out_weight, "ffn_gain": ffn_gain, "expert_ids": expert_ids, "route_weights": route_weights, "gate_up": gate_up, "down_proj": down_proj, "doc_lengths": doc_lengths}


precise = lax.Precision.HIGHEST
epsilon = 1e-05

def segment_of(lengths, positions):
    bounds = jnp.cumsum(lengths).astype(jnp.int32)
    return lax.optimization_barrier(jnp.sum((positions[:, None] >= bounds[None, :]).astype(jnp.int32), axis=1)).astype(jnp.int32)

def span_pass(carry, inputs):
    carry_state, segment_before = carry
    values, step_sizes, log_decay, segment, b_group, c_group = inputs
    length = values.shape[0]
    per_group = values.shape[1] // b_group.shape[1]
    cumulated = jnp.cumsum(log_decay, axis=0)
    row_ids = jnp.arange(length)
    allowed = (row_ids[:, None] >= row_ids[None, :]) & (segment[:, None] == segment[None, :])
    spread = jnp.transpose(cumulated[:, None, :] - cumulated[None, :, :], (2, 0, 1))
    decays = jnp.where(allowed[None], jnp.exp(jnp.minimum(spread, 0.0)), 0.0)
    scores = jnp.einsum('ign,jgn->gij', c_group, b_group, precision=precise)
    scores = jnp.repeat(scores, per_group, axis=0)
    weights = decays * scores * jnp.transpose(step_sizes)[:, None, :]
    inside = jnp.einsum('hij,jhp->ihp', weights, values, precision=precise)
    c_heads = jnp.repeat(c_group, per_group, axis=1)
    b_heads = jnp.repeat(b_group, per_group, axis=1)
    living = (segment == segment_before).astype(jnp.float32)
    reach = living[:, None] * jnp.exp(cumulated)
    carried = jnp.einsum('hpn,ihn->ihp', carry_state, c_heads, precision=precise) * reach[:, :, None]
    final_log = cumulated[-1]
    tail_weight = jnp.where((segment == segment[-1])[:, None], jnp.exp(jnp.minimum(final_log[None, :] - cumulated, 0.0)), 0.0) * step_sizes
    fresh_state = jnp.einsum('jhp,jhn->hpn', values * tail_weight[:, :, None], b_heads, precision=precise)
    keep_factor = (segment[-1] == segment_before).astype(jnp.float32) * jnp.exp(final_log)
    carry_state = keep_factor[:, None, None] * carry_state + fresh_state
    return ((carry_state, segment[-1]), inside + carried)

def run_spans(values, step_sizes, log_decay, segment, b_group, c_group, zero_state, segment_before):
    number = values.shape[0] // SPAN

    def blocked(array):
        return array.reshape((number, SPAN) + array.shape[1:])
    inputs = tuple((blocked(array) for array in (values, step_sizes, log_decay, segment, b_group, c_group)))
    (end_state, ignored), outputs = lax.scan(span_pass, (zero_state, segment_before), inputs)
    return (outputs.reshape(values.shape), end_state)

def gated_norm(mixed_out, gate, gain, groups):
    gated = mixed_out * jax.nn.silu(gate.astype(jnp.float32))
    parts = gated.reshape(gated.shape[0], groups, -1)
    scale = lax.rsqrt(lax.optimization_barrier(jnp.mean(parts * parts, axis=-1, keepdims=True)) + epsilon)
    return ((parts * scale).reshape(gated.shape) * gain[None, :]).astype(jnp.bfloat16)

def reference(hidden_in, mix_values, mix_gate, state_proj, step_raw, step_bias, decay_rate, skip_gain, norm_gain, out_weight, ffn_gain, expert_ids, route_weights, gate_up, down_proj, doc_lengths):
    step_all = jax.nn.softplus(step_raw.astype(jnp.float32) + step_bias[None, :])
    log_all = -step_all * decay_rate[None, :] / SEQ_TOK
    values_all = mix_values.astype(jnp.float32).reshape(N_DP, SEQ_TOK, HEADS, HEADDIM)
    proj_all = state_proj.astype(jnp.float32).reshape(N_DP, SEQ_TOK, GROUPS, 2, STATE)
    positions = jnp.arange(SEQ_TOK, dtype=jnp.int32)

    def group_segments(lengths):
        return segment_of(lengths, positions)
    segments = lax.map(group_segments, doc_lengths)

    def one_group(inputs):
        values, step_sizes, log_decay, segment, projected = inputs
        zero_state = jnp.zeros((HEADS, HEADDIM, STATE), jnp.float32)
        mixed_out, ignored = run_spans(values, step_sizes, log_decay, segment, projected[:, :, 0], projected[:, :, 1], zero_state, jnp.array(-1, jnp.int32))
        return mixed_out
    mixed_all = lax.map(one_group, (values_all, step_all.reshape(N_DP, SEQ_TOK, HEADS), log_all.reshape(N_DP, SEQ_TOK, HEADS), segments, proj_all))
    mixed_all = mixed_all + skip_gain[None, None, :, None] * values_all
    normed_mix = gated_norm(mixed_all.reshape(TOKENS, HEADS * HEADDIM), mix_gate, norm_gain, GROUPS)
    mixer_out = jnp.dot(normed_mix, out_weight, preferred_element_type=jnp.float32)
    merged = lax.optimization_barrier((hidden_in.astype(jnp.float32) + mixer_out).astype(jnp.bfloat16))
    merged_f = merged.astype(jnp.float32)
    square_mean = lax.optimization_barrier(jnp.mean(merged_f * merged_f, axis=-1, keepdims=True))
    normed = (merged_f * lax.rsqrt(square_mean + epsilon) * ffn_gain[None, :]).astype(jnp.bfloat16)
    blocks = TOKENS // TOK_DEV
    per_block = TOK_DEV * TOP
    block_ids = expert_ids.reshape(blocks, per_block)

    def block_rank(ids_block):
        onehot = (ids_block[:, None] == jnp.arange(EXPERTS, dtype=jnp.int32)[None, :]).astype(jnp.int32)
        return lax.optimization_barrier(jnp.sum((jnp.cumsum(onehot, axis=0) - onehot) * onehot, axis=1)).astype(jnp.int32)
    ranks = lax.map(block_rank, block_ids)
    block_index = jnp.arange(blocks, dtype=jnp.int32)[:, None]
    slots = ((block_ids * blocks + block_index) * CAP + ranks).reshape(-1).astype(jnp.int32)
    route_token = jnp.arange(TOKENS * TOP, dtype=jnp.int32) // TOP
    slot_token = jnp.zeros((EXPERTS * blocks * CAP,), jnp.int32).at[slots].set(route_token)
    slot_weight = jnp.zeros((EXPERTS * blocks * CAP,), jnp.float32).at[slots].set(route_weights.reshape(-1))

    def add_expert(total, inputs):
        tokens_here, weight_here, first_proj, second_proj = inputs
        rows_in = normed[tokens_here]
        hidden = jnp.dot(rows_in, first_proj, preferred_element_type=jnp.float32)
        active = (jax.nn.silu(hidden[:, :FF]) * hidden[:, FF:]).astype(jnp.bfloat16)
        result = jnp.dot(active, second_proj, preferred_element_type=jnp.float32).astype(jnp.bfloat16)
        return (total.at[tokens_here].add(weight_here[:, None] * result.astype(jnp.float32)), None)
    total, ignored = lax.scan(add_expert, jnp.zeros((TOKENS, D), jnp.float32), (slot_token.reshape(EXPERTS, -1), slot_weight.reshape(EXPERTS, -1), gate_up, down_proj))
    return (merged_f + total).astype(jnp.bfloat16)
```

```python
import jax
import jax.numpy as jnp
from jax import lax
from jax.experimental import pallas as pl
from jax.experimental.pallas import tpu as pltpu
from jax.sharding import PartitionSpec as P

D = 2048
HEADS = 64
HEADDIM = 64
STATE = 128
GROUPS = 8
FF = 768
TOP = 8
PER = HEADS // GROUPS
WIDE = PER * HEADDIM
CHUNKS = 4

precise = lax.Precision.HIGHEST
epsilon = 1e-05
f32 = jnp.float32
bf16 = jnp.bfloat16


def mix_inside(x_ref, bc_ref, cols_ref, rows_ref, seg_col_ref, seg_row_ref, y_ref, state_ref):
    rows = x_ref.shape[0]
    b = bc_ref[:, :STATE]
    c = bc_ref[:, STATE:]
    scores = lax.dot_general(c, b, (((1,), (1,)), ((), ())), preferred_element_type=f32)
    i = lax.broadcasted_iota(jnp.int32, (rows, rows), 0)
    j = lax.broadcasted_iota(jnp.int32, (rows, rows), 1)
    allowed = (i >= j) & (seg_col_ref[...] == seg_row_ref[...])
    scores = jnp.where(allowed, scores, 0.0)
    low = lax.broadcasted_iota(jnp.int32, (rows, 2 * HEADDIM), 1) < HEADDIM
    cols = cols_ref[0]
    cum_rows = rows_ref[0]
    for pair in range(PER // 2):
        here = pl.ds(pair * 2 * HEADDIM, 2 * HEADDIM)
        h0, h1 = 2 * pair, 2 * pair + 1
        x = x_ref[:, here].astype(f32)
        step = jnp.where(low, cols[:, PER + h0 : PER + h0 + 1], cols[:, PER + h1 : PER + h1 + 1])
        tail = jnp.where(low, cols[:, 2 * PER + h0 : 2 * PER + h0 + 1], cols[:, 2 * PER + h1 : 2 * PER + h1 + 1])
        stepped = (x * step).astype(bf16)
        parts = []
        for h in (h0, h1):
            spread = cols[:, h : h + 1] - cum_rows[h : h + 1, :]
            weights = (jnp.exp(jnp.minimum(spread, 0.0)) * scores).astype(bf16)
            parts.append(jnp.dot(weights, stepped, preferred_element_type=f32))
        y_ref[:, here] = jnp.where(low, parts[0], parts[1])
        state_ref[0, :, here] = lax.dot_general(
            b, (x * tail).astype(bf16), (((0,), (0,)), ((), ())), preferred_element_type=f32
        ).astype(state_ref.dtype)


def mix_finish(y_ref, x_ref, bc_ref, gate_ref, state_ref, reach_ref, skip_ref, gain_ref, out_ref):
    rows = x_ref.shape[0]
    c = bc_ref[:, STATE:]
    carried = jnp.dot(c, state_ref[0], preferred_element_type=f32)
    low = lax.broadcasted_iota(jnp.int32, (rows, 2 * HEADDIM), 1) < HEADDIM
    reach = reach_ref[0]
    total = jnp.zeros((rows, 1), f32)
    parts = []
    for pair in range(PER // 2):
        at = slice(pair * 2 * HEADDIM, (pair + 1) * 2 * HEADDIM)
        h0, h1 = 2 * pair, 2 * pair + 1
        factor = jnp.where(low, reach[:, h0 : h0 + 1], reach[:, h1 : h1 + 1])
        mixed = y_ref[:, at] + carried[:, at] * factor + skip_ref[:, at] * x_ref[:, at].astype(f32)
        u = mixed * jax.nn.silu(gate_ref[:, at].astype(f32))
        total = total + jnp.sum(u * u, axis=1, keepdims=True)
        parts.append(u)
    scale = lax.rsqrt(total / WIDE + epsilon)
    for pair in range(PER // 2):
        at = slice(pair * 2 * HEADDIM, (pair + 1) * 2 * HEADDIM)
        out_ref[:, at] = (parts[pair] * scale * gain_ref[:, at]).astype(bf16)


def mixer(mix_values, mix_gate, state_proj, step_raw, step_bias, decay_rate, skip_gain, norm_gain, lengths):
    rows = mix_values.shape[0]
    seq_size = lax.axis_size("seq")
    rank = lax.axis_index("seq")
    seq_tok = rows * seq_size
    start = rank * rows
    bounds = jnp.cumsum(lengths)
    positions = start + jnp.arange(rows, dtype=jnp.int32)
    segment = jnp.sum((positions[:, None] >= bounds[None, :]).astype(jnp.int32), axis=1)
    before = jnp.where(rank == 0, -1, jnp.sum((start - 1 >= bounds).astype(jnp.int32)))
    last = jnp.sum((start + rows - 1 >= bounds).astype(jnp.int32))
    steps = jax.nn.softplus(step_raw.astype(f32) + step_bias[None, :])
    log_decay = -steps * decay_rate[None, :] / seq_tok
    ids = jnp.arange(rows)
    lower = (ids[:, None] >= ids[None, :]).astype(f32)
    cum = jnp.dot(lower, log_decay, precision=precise)
    final = cum[-1:]
    tail = jnp.where((segment == last)[:, None], jnp.exp(jnp.minimum(final - cum, 0.0)), 0.0) * steps
    reach = (segment == before).astype(f32)[:, None] * jnp.exp(cum)
    keep = (last == before).astype(f32) * jnp.exp(final[0])
    cols = jnp.stack([cum, steps, tail], axis=1).reshape(rows, 3, GROUPS, PER)
    cols = jnp.transpose(cols, (2, 0, 1, 3)).reshape(GROUPS, rows, 3 * PER)
    cum_rows = jnp.transpose(cum).reshape(GROUPS, PER, rows)
    reach = jnp.transpose(reach.reshape(rows, GROUPS, PER), (1, 0, 2))
    wide = pl.BlockSpec((rows, WIDE), lambda g: (0, g))
    proj = pl.BlockSpec((rows, 2 * STATE), lambda g: (0, g))
    vector = pl.BlockSpec((1, WIDE), lambda g: (0, g))
    states = pl.BlockSpec((1, STATE, WIDE), lambda g: (g, 0, 0))
    inside, local = pl.pallas_call(
        mix_inside,
        grid=(GROUPS,),
        in_specs=[
            wide,
            proj,
            pl.BlockSpec((1, rows, 3 * PER), lambda g: (g, 0, 0)),
            pl.BlockSpec((1, PER, rows), lambda g: (g, 0, 0)),
            pl.BlockSpec((rows, 1), lambda g: (0, 0)),
            pl.BlockSpec((1, rows), lambda g: (0, 0)),
        ],
        out_specs=[wide, states],
        out_shape=[
            jax.ShapeDtypeStruct((rows, HEADS * HEADDIM), f32),
            jax.ShapeDtypeStruct((GROUPS, STATE, WIDE), bf16),
        ],
        compiler_params=pltpu.CompilerParams(vmem_limit_bytes=40 * 2**20),
        cost_estimate=pl.CostEstimate(flops=10**10, bytes_accessed=10**7, transcendentals=4 * 10**6),
    )(mix_values, state_proj, cols, cum_rows, segment[:, None], segment[None, :])
    keep_wide = jnp.repeat(keep, HEADDIM).reshape(GROUPS, 1, WIDE)
    width = GROUPS // CHUNKS
    carried = []
    for chunk in range(CHUNKS):
        at = slice(chunk * width, (chunk + 1) * width)
        own, factor = local[at], keep_wide[at]
        total = jnp.zeros(own.shape, bf16)
        for hop in range(seq_size - 1):
            sent = (own.astype(f32) + factor * total.astype(f32)).astype(bf16)
            total = total + lax.ppermute(sent, "seq", [(hop, hop + 1)])
        carried.append(total)
    state_in = jnp.concatenate(carried, axis=0)
    return pl.pallas_call(
        mix_finish,
        grid=(GROUPS,),
        in_specs=[wide, wide, proj, wide, states, pl.BlockSpec((1, rows, PER), lambda g: (g, 0, 0)), vector, vector],
        out_specs=wide,
        out_shape=jax.ShapeDtypeStruct((rows, HEADS * HEADDIM), bf16),
        compiler_params=pltpu.CompilerParams(vmem_limit_bytes=40 * 2**20),
        cost_estimate=pl.CostEstimate(flops=10**9, bytes_accessed=10**7, transcendentals=10**6),
    )(
        inside,
        mix_values,
        state_proj,
        mix_gate,
        state_in,
        reach,
        jnp.repeat(skip_gain, HEADDIM)[None, :],
        norm_gain[None, :],
    )


def experts_of(arrived, gate_up, down_proj):
    hidden = jnp.dot(arrived, gate_up, preferred_element_type=f32)
    active = (jax.nn.silu(hidden[:, :FF]) * hidden[:, FF:]).astype(bf16)
    return jnp.dot(active, down_proj, preferred_element_type=f32).astype(bf16)


def routed(normed, expert_ids, route_weights, gate_up, down_proj):
    rows = normed.shape[0]
    dp_size, seq_size = lax.axis_size("dp"), lax.axis_size("seq")
    rank = lax.axis_index("seq")
    experts = dp_size * seq_size
    capacity = max(2, (9 * rows * TOP + 8 * experts - 1) // (8 * experts))
    all_ids = lax.all_gather(expert_ids, "seq")
    all_weights = lax.all_gather(route_weights, "seq")
    here = jnp.arange(dp_size, dtype=jnp.int32) * seq_size + rank
    hit = all_ids[:, :, :, None] == here
    chosen = jnp.any(hit, axis=2)
    gains = jnp.sum(jnp.where(hit, all_weights[:, :, :, None], 0.0), axis=2)
    ids = jnp.arange(rows)
    earlier = (ids[:, None] > ids[None, :]).astype(bf16)
    place = jnp.einsum("ij,sjd->sid", earlier, chosen.astype(bf16), preferred_element_type=f32)
    place = jnp.where(chosen, place, -1.0)
    slots = jnp.arange(capacity, dtype=jnp.int32).astype(f32)
    current = normed
    arrivals, spreads = [], []
    for offset in range(seq_size):
        source = lax.rem(rank - offset + seq_size, seq_size)
        place_here = lax.dynamic_index_in_dim(place, source, 0, keepdims=False)
        gains_here = lax.dynamic_index_in_dim(gains, source, 0, keepdims=False)
        taken = jnp.transpose(place_here)[:, None, :] == slots[None, :, None]
        outgoing = jnp.dot(
            taken.astype(bf16).reshape(dp_size * capacity, rows), current, preferred_element_type=f32
        ).astype(bf16)
        spread = jnp.where(place_here[:, :, None] == slots, gains_here[:, :, None], 0.0)
        spreads.append(spread.astype(bf16).reshape(rows, dp_size * capacity))
        if offset < seq_size - 1:
            current = lax.ppermute(current, "seq", [(i, (i + 1) % seq_size) for i in range(seq_size)])
        arrivals.append(
            lax.all_to_all(outgoing.reshape(dp_size, capacity, D), "dp", split_axis=0, concat_axis=0, tiled=True)
        )
    total = None
    for offset in list(range(1, seq_size)) + [0]:
        result = experts_of(arrivals[offset].reshape(-1, D), gate_up[0], down_proj[0])
        returned = lax.all_to_all(
            result.reshape(dp_size, capacity, D), "dp", split_axis=0, concat_axis=0, tiled=True
        )
        part = jnp.dot(spreads[offset], returned.reshape(-1, D), preferred_element_type=f32)
        if offset:
            part = lax.ppermute(
                part.astype(bf16), "seq", [(i, (i - offset) % seq_size) for i in range(seq_size)]
            ).astype(f32)
        total = part if total is None else total + part
    return total


def body(
    hidden_in,
    mix_values,
    mix_gate,
    state_proj,
    step_raw,
    step_bias,
    decay_rate,
    skip_gain,
    norm_gain,
    out_weight,
    ffn_gain,
    expert_ids,
    route_weights,
    gate_up,
    down_proj,
    doc_lengths,
):
    dp_size = lax.axis_size("dp")
    share = out_weight.shape[0] // dp_size
    own = lax.dynamic_slice_in_dim(out_weight, lax.axis_index("dp") * share, share)
    weight = lax.all_gather(own, ("seq", "dp"), tiled=True)
    normed_mix = mixer(
        mix_values, mix_gate, state_proj, step_raw, step_bias, decay_rate, skip_gain, norm_gain, doc_lengths[0]
    )
    mixer_out = jnp.dot(normed_mix, weight, preferred_element_type=f32)
    merged = lax.optimization_barrier((hidden_in.astype(f32) + mixer_out).astype(bf16))
    merged_f = merged.astype(f32)
    square_mean = jnp.mean(merged_f * merged_f, axis=-1, keepdims=True)
    normed = (merged_f * lax.rsqrt(square_mean + epsilon) * ffn_gain[None, :]).astype(bf16)
    moe_out = routed(normed, expert_ids, route_weights, gate_up, down_proj)
    return (merged_f + moe_out).astype(bf16)


def solution(mesh):
    both = P(("dp", "seq"), None)
    deep = P(("dp", "seq"), None, None)
    in_specs = (both, both, both, both, both, P(), P(), P(), P(), P("seq", None), P(), both, both, deep, deep, P("dp", None))
    return jax.shard_map(body, mesh=mesh, in_specs=in_specs, out_specs=both, check_vma=False)
```

```python
import jax
import jax.numpy as jnp
from jax import lax
from jax.experimental import pallas as pl
from jax.experimental.pallas import tpu as pltpu
from jax.sharding import PartitionSpec as P

D = 2048
HEADS = 64
HEADDIM = 64
STATE = 128
GROUPS = 8
FF = 768
TOP = 8
PER = HEADS // GROUPS
WIDE = PER * HEADDIM
CHUNKS = 4

precise = lax.Precision.HIGHEST
epsilon = 1e-05
f32 = jnp.float32
bf16 = jnp.bfloat16


def mix_inside(x_ref, bc_ref, cols_ref, rows_ref, seg_col_ref, seg_row_ref, y_ref, state_ref):
    rows = x_ref.shape[0]
    b = bc_ref[:, :STATE]
    c = bc_ref[:, STATE:]
    scores = lax.dot_general(c, b, (((1,), (1,)), ((), ())), preferred_element_type=f32)
    i = lax.broadcasted_iota(jnp.int32, (rows, rows), 0)
    j = lax.broadcasted_iota(jnp.int32, (rows, rows), 1)
    allowed = (i >= j) & (seg_col_ref[...] == seg_row_ref[...])
    scores = jnp.where(allowed, scores, 0.0)
    low = lax.broadcasted_iota(jnp.int32, (rows, 2 * HEADDIM), 1) < HEADDIM
    cols = cols_ref[0]
    cum_rows = rows_ref[0]
    for pair in range(PER // 2):
        here = pl.ds(pair * 2 * HEADDIM, 2 * HEADDIM)
        h0, h1 = 2 * pair, 2 * pair + 1
        x = x_ref[:, here].astype(f32)
        step = jnp.where(low, cols[:, PER + h0 : PER + h0 + 1], cols[:, PER + h1 : PER + h1 + 1])
        tail = jnp.where(low, cols[:, 2 * PER + h0 : 2 * PER + h0 + 1], cols[:, 2 * PER + h1 : 2 * PER + h1 + 1])
        stepped = (x * step).astype(bf16)
        parts = []
        for h in (h0, h1):
            spread = cols[:, h : h + 1] - cum_rows[h : h + 1, :]
            weights = (jnp.exp(jnp.minimum(spread, 0.0)) * scores).astype(bf16)
            parts.append(jnp.dot(weights, stepped, preferred_element_type=f32))
        y_ref[:, here] = jnp.where(low, parts[0], parts[1])
        state_ref[0, :, here] = lax.dot_general(
            b, (x * tail).astype(bf16), (((0,), (0,)), ((), ())), preferred_element_type=f32
        ).astype(state_ref.dtype)


def mix_finish(y_ref, x_ref, bc_ref, gate_ref, state_ref, reach_ref, skip_ref, gain_ref, out_ref):
    rows = x_ref.shape[0]
    c = bc_ref[:, STATE:]
    carried = jnp.dot(c, state_ref[0], preferred_element_type=f32)
    low = lax.broadcasted_iota(jnp.int32, (rows, 2 * HEADDIM), 1) < HEADDIM
    reach = reach_ref[0]
    total = jnp.zeros((rows, 1), f32)
    parts = []
    for pair in range(PER // 2):
        at = slice(pair * 2 * HEADDIM, (pair + 1) * 2 * HEADDIM)
        h0, h1 = 2 * pair, 2 * pair + 1
        factor = jnp.where(low, reach[:, h0 : h0 + 1], reach[:, h1 : h1 + 1])
        mixed = y_ref[:, at] + carried[:, at] * factor + skip_ref[:, at] * x_ref[:, at].astype(f32)
        u = mixed * jax.nn.silu(gate_ref[:, at].astype(f32))
        total = total + jnp.sum(u * u, axis=1, keepdims=True)
        parts.append(u)
    scale = lax.rsqrt(total / WIDE + epsilon)
    for pair in range(PER // 2):
        at = slice(pair * 2 * HEADDIM, (pair + 1) * 2 * HEADDIM)
        out_ref[:, at] = (parts[pair] * scale * gain_ref[:, at]).astype(bf16)


def mixer(mix_values, mix_gate, state_proj, step_raw, step_bias, decay_rate, skip_gain, norm_gain, lengths):
    rows = mix_values.shape[0]
    seq_size = lax.axis_size("seq")
    rank = lax.axis_index("seq")
    seq_tok = rows * seq_size
    start = rank * rows
    bounds = jnp.cumsum(lengths)
    positions = start + jnp.arange(rows, dtype=jnp.int32)
    segment = jnp.sum((positions[:, None] >= bounds[None, :]).astype(jnp.int32), axis=1)
    before = jnp.where(rank == 0, -1, jnp.sum((start - 1 >= bounds).astype(jnp.int32)))
    last = jnp.sum((start + rows - 1 >= bounds).astype(jnp.int32))
    steps = jax.nn.softplus(step_raw.astype(f32) + step_bias[None, :])
    log_decay = -steps * decay_rate[None, :] / seq_tok
    ids = jnp.arange(rows)
    lower = (ids[:, None] >= ids[None, :]).astype(f32)
    cum = jnp.dot(lower, log_decay, precision=precise)
    final = cum[-1:]
    tail = jnp.where((segment == last)[:, None], jnp.exp(jnp.minimum(final - cum, 0.0)), 0.0) * steps
    reach = (segment == before).astype(f32)[:, None] * jnp.exp(cum)
    keep = (last == before).astype(f32) * jnp.exp(final[0])
    cols = jnp.stack([cum, steps, tail], axis=1).reshape(rows, 3, GROUPS, PER)
    cols = jnp.transpose(cols, (2, 0, 1, 3)).reshape(GROUPS, rows, 3 * PER)
    cum_rows = jnp.transpose(cum).reshape(GROUPS, PER, rows)
    reach = jnp.transpose(reach.reshape(rows, GROUPS, PER), (1, 0, 2))
    wide = pl.BlockSpec((rows, WIDE), lambda g: (0, g))
    proj = pl.BlockSpec((rows, 2 * STATE), lambda g: (0, g))
    vector = pl.BlockSpec((1, WIDE), lambda g: (0, g))
    states = pl.BlockSpec((1, STATE, WIDE), lambda g: (g, 0, 0))
    inside, local = pl.pallas_call(
        mix_inside,
        grid=(GROUPS,),
        in_specs=[
            wide,
            proj,
            pl.BlockSpec((1, rows, 3 * PER), lambda g: (g, 0, 0)),
            pl.BlockSpec((1, PER, rows), lambda g: (g, 0, 0)),
            pl.BlockSpec((rows, 1), lambda g: (0, 0)),
            pl.BlockSpec((1, rows), lambda g: (0, 0)),
        ],
        out_specs=[wide, states],
        out_shape=[
            jax.ShapeDtypeStruct((rows, HEADS * HEADDIM), f32),
            jax.ShapeDtypeStruct((GROUPS, STATE, WIDE), bf16),
        ],
        compiler_params=pltpu.CompilerParams(vmem_limit_bytes=40 * 2**20),
        cost_estimate=pl.CostEstimate(flops=10**10, bytes_accessed=10**7, transcendentals=4 * 10**6),
    )(mix_values, state_proj, cols, cum_rows, segment[:, None], segment[None, :])
    keep_wide = jnp.repeat(keep, HEADDIM).reshape(GROUPS, 1, WIDE)
    width = GROUPS // CHUNKS
    carried = []
    for chunk in range(CHUNKS):
        at = slice(chunk * width, (chunk + 1) * width)
        own, factor = local[at], keep_wide[at]
        total = jnp.zeros(own.shape, bf16)
        for hop in range(seq_size - 1):
            sent = (own.astype(f32) + factor * total.astype(f32)).astype(bf16)
            total = total + lax.ppermute(sent, "seq", [(hop, hop + 1)])
        carried.append(total)
    state_in = jnp.concatenate(carried, axis=0)
    return pl.pallas_call(
        mix_finish,
        grid=(GROUPS,),
        in_specs=[wide, wide, proj, wide, states, pl.BlockSpec((1, rows, PER), lambda g: (g, 0, 0)), vector, vector],
        out_specs=wide,
        out_shape=jax.ShapeDtypeStruct((rows, HEADS * HEADDIM), bf16),
        compiler_params=pltpu.CompilerParams(vmem_limit_bytes=40 * 2**20),
        cost_estimate=pl.CostEstimate(flops=10**9, bytes_accessed=10**7, transcendentals=10**6),
    )(
        inside,
        mix_values,
        state_proj,
        mix_gate,
        state_in,
        reach,
        jnp.repeat(skip_gain, HEADDIM)[None, :],
        norm_gain[None, :],
    )


def experts_of(arrived, gate_up, down_proj):
    hidden = jnp.dot(arrived, gate_up, preferred_element_type=f32)
    active = (jax.nn.silu(hidden[:, :FF]) * hidden[:, FF:]).astype(bf16)
    return jnp.dot(active, down_proj, preferred_element_type=f32).astype(bf16)


def routed(normed, expert_ids, route_weights, gate_up, down_proj):
    rows = normed.shape[0]
    dp_size, seq_size = lax.axis_size("dp"), lax.axis_size("seq")
    rank = lax.axis_index("seq")
    experts = dp_size * seq_size
    capacity = max(2, (9 * rows * TOP + 8 * experts - 1) // (8 * experts))
    ring = [(i, (i + 1) % seq_size) for i in range(seq_size)]
    routes = [jnp.concatenate([expert_ids.T.astype(f32), route_weights.T], axis=0)]
    for _ in range(seq_size - 1):
        routes.append(lax.ppermute(routes[-1], "seq", ring))
    routes = jnp.stack(routes)
    all_ids = jnp.transpose(routes[:, :TOP], (0, 2, 1)).astype(jnp.int32)
    all_weights = jnp.transpose(routes[:, TOP:], (0, 2, 1))
    here = jnp.arange(dp_size, dtype=jnp.int32) * seq_size + rank
    hit = all_ids[:, :, :, None] == here
    chosen = jnp.any(hit, axis=2)
    gains = jnp.sum(jnp.where(hit, all_weights[:, :, :, None], 0.0), axis=2)
    ids = jnp.arange(rows)
    earlier = (ids[:, None] > ids[None, :]).astype(bf16)
    place = jnp.einsum("ij,sjd->sid", earlier, chosen.astype(bf16), preferred_element_type=f32)
    place = jnp.where(chosen, place, -1.0)
    slots = jnp.arange(capacity, dtype=jnp.int32).astype(f32)
    current = normed
    arrivals, spreads = [], []
    for offset in range(seq_size):
        place_here = place[offset]
        gains_here = gains[offset]
        taken = jnp.transpose(place_here)[:, None, :] == slots[None, :, None]
        outgoing = jnp.dot(
            taken.astype(bf16).reshape(dp_size * capacity, rows), current, preferred_element_type=f32
        ).astype(bf16)
        spread = jnp.where(place_here[:, :, None] == slots, gains_here[:, :, None], 0.0)
        spreads.append(spread.astype(bf16).reshape(rows, dp_size * capacity))
        if offset < seq_size - 1:
            current = lax.ppermute(current, "seq", ring)
        arrivals.append(
            lax.all_to_all(outgoing.reshape(dp_size, capacity, D), "dp", split_axis=0, concat_axis=0, tiled=True)
        )
    order = list(range(1, seq_size)) + [0]
    parts = []
    total = None
    for turn, offset in enumerate(order):
        arrived = arrivals[offset]
        if turn >= 2:
            arrived, parts[turn - 2] = lax.optimization_barrier((arrived, parts[turn - 2]))
        result = experts_of(arrived.reshape(-1, D), gate_up[0], down_proj[0])
        returned = lax.all_to_all(
            result.reshape(dp_size, capacity, D), "dp", split_axis=0, concat_axis=0, tiled=True
        )
        part = jnp.dot(spreads[offset], returned.reshape(-1, D), preferred_element_type=f32)
        parts.append(part.astype(bf16) if offset else part)
    for turn, offset in enumerate(order):
        part = parts[turn]
        if offset:
            part = lax.ppermute(part, "seq", [(i, (i - offset) % seq_size) for i in range(seq_size)]).astype(f32)
        total = part if total is None else total + part
    return total


def body(
    hidden_in,
    mix_values,
    mix_gate,
    state_proj,
    step_raw,
    step_bias,
    decay_rate,
    skip_gain,
    norm_gain,
    out_weight,
    ffn_gain,
    expert_ids,
    route_weights,
    gate_up,
    down_proj,
    doc_lengths,
):
    dp_size = lax.axis_size("dp")
    share = out_weight.shape[0] // dp_size
    own = lax.dynamic_slice_in_dim(out_weight, lax.axis_index("dp") * share, share)
    weight = lax.all_gather(own, ("seq", "dp"), tiled=True)
    normed_mix = mixer(
        mix_values, mix_gate, state_proj, step_raw, step_bias, decay_rate, skip_gain, norm_gain, doc_lengths[0]
    )
    mixer_out = jnp.dot(normed_mix, weight, preferred_element_type=f32)
    merged = lax.optimization_barrier((hidden_in.astype(f32) + mixer_out).astype(bf16))
    merged_f = merged.astype(f32)
    square_mean = jnp.mean(merged_f * merged_f, axis=-1, keepdims=True)
    normed = (merged_f * lax.rsqrt(square_mean + epsilon) * ffn_gain[None, :]).astype(bf16)
    moe_out = routed(normed, expert_ids, route_weights, gate_up, down_proj)
    return (merged_f + moe_out).astype(bf16)


def solution(mesh):
    both = P(("dp", "seq"), None)
    deep = P(("dp", "seq"), None, None)
    in_specs = (both, both, both, both, both, P(), P(), P(), P(), P("seq", None), P(), both, both, deep, deep, P("dp", None))
    return jax.shard_map(body, mesh=mesh, in_specs=in_specs, out_specs=both, check_vma=False)
```

```python
import jax
import jax.numpy as jnp
from jax import lax
from jax.experimental import pallas as pl
from jax.experimental.pallas import tpu as pltpu
from jax.sharding import PartitionSpec as P

D = 2048
HEADS = 64
HEADDIM = 64
STATE = 128
GROUPS = 8
FF = 768
TOP = 8
PER = HEADS // GROUPS
WIDE = PER * HEADDIM
CHUNKS = 4

precise = lax.Precision.HIGHEST
epsilon = 1e-05
f32 = jnp.float32
bf16 = jnp.bfloat16


def mix_inside(x_ref, bc_ref, cols_ref, rows_ref, seg_col_ref, seg_row_ref, y_ref, state_ref):
    rows = x_ref.shape[0]
    b = bc_ref[:, :STATE]
    c = bc_ref[:, STATE:]
    scores = lax.dot_general(c, b, (((1,), (1,)), ((), ())), preferred_element_type=f32)
    i = lax.broadcasted_iota(jnp.int32, (rows, rows), 0)
    j = lax.broadcasted_iota(jnp.int32, (rows, rows), 1)
    allowed = (i >= j) & (seg_col_ref[...] == seg_row_ref[...])
    scores = jnp.where(allowed, scores, 0.0)
    low = lax.broadcasted_iota(jnp.int32, (rows, 2 * HEADDIM), 1) < HEADDIM
    cols = cols_ref[0]
    cum_rows = rows_ref[0]
    for pair in range(PER // 2):
        here = pl.ds(pair * 2 * HEADDIM, 2 * HEADDIM)
        h0, h1 = 2 * pair, 2 * pair + 1
        x = x_ref[:, here].astype(f32)
        step = jnp.where(low, cols[:, PER + h0 : PER + h0 + 1], cols[:, PER + h1 : PER + h1 + 1])
        tail = jnp.where(low, cols[:, 2 * PER + h0 : 2 * PER + h0 + 1], cols[:, 2 * PER + h1 : 2 * PER + h1 + 1])
        stepped = (x * step).astype(bf16)
        parts = []
        for h in (h0, h1):
            spread = cols[:, h : h + 1] - cum_rows[h : h + 1, :]
            weights = (jnp.exp(jnp.minimum(spread, 0.0)) * scores).astype(bf16)
            parts.append(jnp.dot(weights, stepped, preferred_element_type=f32))
        y_ref[:, here] = jnp.where(low, parts[0], parts[1])
        state_ref[0, :, here] = lax.dot_general(
            b, (x * tail).astype(bf16), (((0,), (0,)), ((), ())), preferred_element_type=f32
        ).astype(state_ref.dtype)


def mix_finish(y_ref, x_ref, bc_ref, gate_ref, state_ref, reach_ref, skip_ref, gain_ref, out_ref):
    rows = x_ref.shape[0]
    c = bc_ref[:, STATE:]
    carried = jnp.dot(c, state_ref[0], preferred_element_type=f32)
    low = lax.broadcasted_iota(jnp.int32, (rows, 2 * HEADDIM), 1) < HEADDIM
    reach = reach_ref[0]
    total = jnp.zeros((rows, 1), f32)
    parts = []
    for pair in range(PER // 2):
        at = slice(pair * 2 * HEADDIM, (pair + 1) * 2 * HEADDIM)
        h0, h1 = 2 * pair, 2 * pair + 1
        factor = jnp.where(low, reach[:, h0 : h0 + 1], reach[:, h1 : h1 + 1])
        mixed = y_ref[:, at] + carried[:, at] * factor + skip_ref[:, at] * x_ref[:, at].astype(f32)
        u = mixed * jax.nn.silu(gate_ref[:, at].astype(f32))
        total = total + jnp.sum(u * u, axis=1, keepdims=True)
        parts.append(u)
    scale = lax.rsqrt(total / WIDE + epsilon)
    for pair in range(PER // 2):
        at = slice(pair * 2 * HEADDIM, (pair + 1) * 2 * HEADDIM)
        out_ref[:, at] = (parts[pair] * scale * gain_ref[:, at]).astype(bf16)


def mixer(mix_values, mix_gate, state_proj, step_raw, step_bias, decay_rate, skip_gain, norm_gain, lengths):
    rows = mix_values.shape[0]
    seq_size = lax.axis_size("seq")
    rank = lax.axis_index("seq")
    seq_tok = rows * seq_size
    start = rank * rows
    bounds = jnp.cumsum(lengths)
    positions = start + jnp.arange(rows, dtype=jnp.int32)
    segment = jnp.sum((positions[:, None] >= bounds[None, :]).astype(jnp.int32), axis=1)
    before = jnp.where(rank == 0, -1, jnp.sum((start - 1 >= bounds).astype(jnp.int32)))
    last = jnp.sum((start + rows - 1 >= bounds).astype(jnp.int32))
    steps = jax.nn.softplus(step_raw.astype(f32) + step_bias[None, :])
    log_decay = -steps * decay_rate[None, :] / seq_tok
    ids = jnp.arange(rows)
    lower = (ids[:, None] >= ids[None, :]).astype(f32)
    cum = jnp.dot(lower, log_decay, precision=precise)
    final = cum[-1:]
    tail = jnp.where((segment == last)[:, None], jnp.exp(jnp.minimum(final - cum, 0.0)), 0.0) * steps
    reach = (segment == before).astype(f32)[:, None] * jnp.exp(cum)
    keep = (last == before).astype(f32) * jnp.exp(final[0])
    cols = jnp.stack([cum, steps, tail], axis=1).reshape(rows, 3, GROUPS, PER)
    cols = jnp.transpose(cols, (2, 0, 1, 3)).reshape(GROUPS, rows, 3 * PER)
    cum_rows = jnp.transpose(cum).reshape(GROUPS, PER, rows)
    reach = jnp.transpose(reach.reshape(rows, GROUPS, PER), (1, 0, 2))
    wide = pl.BlockSpec((rows, WIDE), lambda g: (0, g))
    proj = pl.BlockSpec((rows, 2 * STATE), lambda g: (0, g))
    vector = pl.BlockSpec((1, WIDE), lambda g: (0, g))
    states = pl.BlockSpec((1, STATE, WIDE), lambda g: (g, 0, 0))
    inside, local = pl.pallas_call(
        mix_inside,
        grid=(GROUPS,),
        in_specs=[
            wide,
            proj,
            pl.BlockSpec((1, rows, 3 * PER), lambda g: (g, 0, 0)),
            pl.BlockSpec((1, PER, rows), lambda g: (g, 0, 0)),
            pl.BlockSpec((rows, 1), lambda g: (0, 0)),
            pl.BlockSpec((1, rows), lambda g: (0, 0)),
        ],
        out_specs=[wide, states],
        out_shape=[
            jax.ShapeDtypeStruct((rows, HEADS * HEADDIM), f32),
            jax.ShapeDtypeStruct((GROUPS, STATE, WIDE), bf16),
        ],
        compiler_params=pltpu.CompilerParams(vmem_limit_bytes=40 * 2**20),
        cost_estimate=pl.CostEstimate(flops=10**10, bytes_accessed=10**7, transcendentals=4 * 10**6),
    )(mix_values, state_proj, cols, cum_rows, segment[:, None], segment[None, :])
    keep_wide = jnp.repeat(keep, HEADDIM).reshape(GROUPS, 1, WIDE)
    width = GROUPS // CHUNKS
    carried = []
    for chunk in range(CHUNKS):
        at = slice(chunk * width, (chunk + 1) * width)
        own, factor = local[at], keep_wide[at]
        total = jnp.zeros(own.shape, bf16)
        for hop in range(seq_size - 1):
            sent = (own.astype(f32) + factor * total.astype(f32)).astype(bf16)
            total = total + lax.ppermute(sent, "seq", [(hop, hop + 1)])
        carried.append(total)
    state_in = jnp.concatenate(carried, axis=0)
    return pl.pallas_call(
        mix_finish,
        grid=(GROUPS,),
        in_specs=[wide, wide, proj, wide, states, pl.BlockSpec((1, rows, PER), lambda g: (g, 0, 0)), vector, vector],
        out_specs=wide,
        out_shape=jax.ShapeDtypeStruct((rows, HEADS * HEADDIM), bf16),
        compiler_params=pltpu.CompilerParams(vmem_limit_bytes=40 * 2**20),
        cost_estimate=pl.CostEstimate(flops=10**9, bytes_accessed=10**7, transcendentals=10**6),
    )(
        inside,
        mix_values,
        state_proj,
        mix_gate,
        state_in,
        reach,
        jnp.repeat(skip_gain, HEADDIM)[None, :],
        norm_gain[None, :],
    )


def swap(rows):
    dp_size = lax.axis_size("dp")
    blocks = rows.reshape(dp_size, -1, rows.shape[-1])
    return lax.all_to_all(blocks, "dp", split_axis=0, concat_axis=0, tiled=True).reshape(rows.shape)


def active_of(arrived, gate_up):
    hidden = jnp.dot(arrived, gate_up, preferred_element_type=f32)
    return (jax.nn.silu(hidden[:, :FF]) * hidden[:, FF:]).astype(bf16)


def taken_by(place, slots):
    return (jnp.transpose(place)[:, None, :] == slots[None, :, None]).astype(bf16).reshape(-1, place.shape[0])


def spread_by(place, gains, slots):
    return jnp.where(place[:, :, None] == slots, gains[:, :, None], 0.0).astype(bf16).reshape(place.shape[0], -1)


def routed(normed, expert_ids, route_weights, gate_up, down_proj):
    rows = normed.shape[0]
    dp_size, seq_size = lax.axis_size("dp"), lax.axis_size("seq")
    rank = lax.axis_index("seq")
    experts = dp_size * seq_size
    capacity = max(2, (9 * rows * TOP + 8 * experts - 1) // (8 * experts))
    ring = [(i, (i + 1) % seq_size) for i in range(seq_size)]
    routes = [jnp.concatenate([expert_ids.T.astype(f32), route_weights.T], axis=0)]
    for _ in range(seq_size - 1):
        routes.append(lax.ppermute(routes[-1], "seq", ring))
    routes = jnp.roll(jnp.stack(routes[::-1]), rank + 1, axis=0)
    all_ids = jnp.transpose(routes[:, :TOP], (0, 2, 1)).astype(jnp.int32)
    all_weights = jnp.transpose(routes[:, TOP:], (0, 2, 1))
    here = jnp.arange(dp_size, dtype=jnp.int32) * seq_size + rank
    hit = all_ids[:, :, :, None] == here
    chosen = jnp.any(hit, axis=2)
    gains = jnp.sum(jnp.where(hit, all_weights[:, :, :, None], 0.0), axis=2)
    ids = jnp.arange(rows)
    earlier = (ids[:, None] > ids[None, :]).astype(bf16)
    place = jnp.einsum("ij,sjd->sid", earlier, chosen.astype(bf16), preferred_element_type=f32)
    place = jnp.where(chosen, place, -1.0)
    own_place = lax.dynamic_index_in_dim(place, rank, 0, keepdims=False)
    own_gains = lax.dynamic_index_in_dim(gains, rank, 0, keepdims=False)
    ahead = lax.rem(rank - jnp.arange(seq_size) + seq_size, seq_size) - 1
    base = (ahead * capacity).astype(f32)[:, None, None]
    place = jnp.where(chosen & (ahead >= 0)[:, None, None], place + base, -1.0).reshape(-1, dp_size)
    gains = gains.reshape(-1, dp_size)
    own_slots = jnp.arange(capacity, dtype=jnp.int32).astype(f32)
    slots = jnp.arange((seq_size - 1) * capacity, dtype=jnp.int32).astype(f32)

    tokens = lax.all_gather(normed, "seq", tiled=True)
    own_out = jnp.dot(taken_by(own_place, own_slots), normed, preferred_element_type=f32).astype(bf16)
    own_active = active_of(swap(own_out), gate_up[0])
    own_result = jnp.dot(own_active, down_proj[0], preferred_element_type=f32).astype(bf16)
    own_back = swap(own_result)
    tokens, own_back = lax.optimization_barrier((tokens, own_back))

    outgoing = jnp.dot(taken_by(place, slots), tokens, preferred_element_type=f32).astype(bf16)
    active = active_of(swap(outgoing), gate_up[0])
    spread = spread_by(place, gains, slots)
    sums = []
    half = D // 2
    for at in (slice(0, half), slice(half, D)):
        result = jnp.dot(active, down_proj[0][:, at], preferred_element_type=f32).astype(bf16)
        part = jnp.dot(spread, swap(result), preferred_element_type=f32).astype(bf16)
        sums.append(lax.psum_scatter(part, "seq", scatter_dimension=0, tiled=True))
    own = jnp.dot(spread_by(own_place, own_gains, own_slots), own_back, preferred_element_type=f32)
    return own + jnp.concatenate(sums, axis=1).astype(f32)


def body(
    hidden_in,
    mix_values,
    mix_gate,
    state_proj,
    step_raw,
    step_bias,
    decay_rate,
    skip_gain,
    norm_gain,
    out_weight,
    ffn_gain,
    expert_ids,
    route_weights,
    gate_up,
    down_proj,
    doc_lengths,
):
    dp_size = lax.axis_size("dp")
    share = out_weight.shape[0] // dp_size
    own = lax.dynamic_slice_in_dim(out_weight, lax.axis_index("dp") * share, share)
    weight = lax.all_gather(own, ("seq", "dp"), tiled=True)
    normed_mix = mixer(
        mix_values, mix_gate, state_proj, step_raw, step_bias, decay_rate, skip_gain, norm_gain, doc_lengths[0]
    )
    mixer_out = jnp.dot(normed_mix, weight, preferred_element_type=f32)
    merged = lax.optimization_barrier((hidden_in.astype(f32) + mixer_out).astype(bf16))
    merged_f = merged.astype(f32)
    square_mean = jnp.mean(merged_f * merged_f, axis=-1, keepdims=True)
    normed = (merged_f * lax.rsqrt(square_mean + epsilon) * ffn_gain[None, :]).astype(bf16)
    moe_out = routed(normed, expert_ids, route_weights, gate_up, down_proj)
    return (merged_f + moe_out).astype(bf16)


def solution(mesh):
    both = P(("dp", "seq"), None)
    deep = P(("dp", "seq"), None, None)
    in_specs = (both, both, both, both, both, P(), P(), P(), P(), P("seq", None), P(), both, both, deep, deep, P("dp", None))
    return jax.shard_map(body, mesh=mesh, in_specs=in_specs, out_specs=both, check_vma=False)
```
